32 devices in a mesh: parts: 2 (over x), wide: 16 (over z, y, core).
Axes of the slice: x: 2, y: 2, z: 4, core: 2. Of those that a mesh axis runs over, the one named last changes fastest.
Arguments:
- history: bfloat16 [2048, 8, 1024], P(('parts', 'wide')), parts along dimension 0, may hold values from -6 to 6
- pool: bfloat16 [512, 1024], P(('parts', 'wide')), parts along dimension 0, may hold values from -6 to 6
- cand_ids: int32 [64, 128], P(('parts', 'wide')), parts along dimension 0, may hold values from 0 to 255
- block_user: int32 [32, 64], P('parts'), parts along dimension 0, may hold values from 0 to 31, as said below
- norm_gain: float32 [1024], replicated, may hold values from 0.5 to 1.5
- w_in: bfloat16 [1024, 4096], replicated, may hold values from -0.1875 to 0.1875
- attn_gain: float32 [1024], replicated, may hold values from 0.25 to 1.75
- w_out: bfloat16 [1024, 1024], replicated, may hold values from -0.1875 to 0.1875
Outputs:
- scored: bfloat16 [64, 128, 1024], P(('parts', 'wide')), parts along dimension 0
The draws below stay inside these ranges and needn't reach their ends.
There are 2 independent parts, one for each index of `parts`. The reference program is written for one: setup_inputs(seed, part) draws one part's arguments, and reference() takes and returns one part's arrays. A program takes and returns all parts, laid end to end along the dimension named above; an argument that names none is the same for every part. Nothing has to cross between parts.
Inputs may be any that keep to these rules, and one draw needn't show every extreme that they name: `block_user`: user u is ranked on device u // 2. At most 8 blocks of one owner belong to users ranked on one device; every draw reaches this, and some device receives 8 blocks from every owner.
All inputs are finite; a program needn't handle non-finite values.
Results may differ from the reference program's by a relative error of at most 0.0051.
Values may be sent and summed in bfloat16 or wider, within the bound.
A program may use at most 64 MiB of HBM per device.

```python
import jax
import jax.numpy as jnp
from jax import lax

D = 1024
HEADS = 8
BLOCK_ROWS = 8
USERS_DEV = 2
CAND_USER = 128
CACHE_DEV = 64
SLOT = 8
USERS = 32
BLOCKS = 1024
POOL = 256
N_WIDE = 16


def draw_block_user(key, part):
    keys = jax.random.split(key, 5)
    ranker_ids = jnp.arange(N_WIDE, dtype=jnp.int32)
    noise = jax.random.randint(keys[0], (N_WIDE, N_WIDE), 0, N_WIDE, dtype=jnp.int32)
    bias = jax.random.randint(keys[1], (N_WIDE,), 0, 4, dtype=jnp.int32)
    hottest = jax.random.randint(keys[2], (), 0, N_WIDE, dtype=jnp.int32)
    bias = jnp.where(ranker_ids == hottest, 8, bias)
    score = (noise + bias[None, :] * (N_WIDE // 2 + 1)) * N_WIDE + ranker_ids[None, :]
    ranked = jnp.argsort(-score, axis=1, stable=True)
    chosen = ranked[:, :CACHE_DEV // SLOT]
    target = jnp.repeat(chosen, SLOT, axis=1)
    local_user = jax.random.randint(keys[3], (N_WIDE, CACHE_DEV), 0, USERS_DEV, dtype=jnp.int32)
    owner_user = target * USERS_DEV + local_user
    block_ids = jnp.arange(CACHE_DEV, dtype=jnp.int32)
    shuffle_key = jax.random.randint(keys[4], (N_WIDE, CACHE_DEV), 0, CACHE_DEV, dtype=jnp.int32) * CACHE_DEV + block_ids[None, :]
    shuffle = jnp.argsort(shuffle_key, axis=1, stable=True)
    return jnp.take_along_axis(owner_user, shuffle, axis=1).astype(jnp.int32)


def place_ends(array, key, least, high):
    dims = array.shape
    place = [jax.random.randint(jax.random.fold_in(key, axis), (), 0, dims[axis]) for axis in range(len(dims))]
    array = array.at[tuple(place)].set(least)
    longest = dims.index(max(dims))
    place[longest] = (place[longest] + 1) % dims[longest]
    return array.at[tuple(place)].set(high)


def levels(stream_key, extent, cuts, least, largest):
    level = 1.0
    for position, shards_of in cuts:
        draws = jax.random.uniform(jax.random.fold_in(jax.random.fold_in(stream_key, 6), position), (shards_of,), jnp.float32, least / len(cuts), largest / len(cuts))
        level = level * jnp.repeat(jnp.exp(draws), extent[position] // shards_of).reshape((-1,) + (1,) * (len(extent) - 1 - position))
    return level


def normal_values(stream_key, extent, deviation, bound, shards=(), kind=jnp.bfloat16):
    entries = jax.random.normal(stream_key, extent, jnp.float32) * deviation
    if len(shards) > 0:
        entries = levels(stream_key, extent, shards, -0.22, 0.18) * entries
    return jnp.clip(entries, min=-bound, max=bound).astype(kind)


def setup_inputs(seed: int = 0, part: int = 0) -> dict:
    splits = jax.random.split(jax.random.key(seed), 9)
    part_keys = jax.random.split(jax.random.fold_in(splits[8], part), 9)
    history = normal_values(part_keys[0], (BLOCKS, BLOCK_ROWS, D), 1.0, 6.0, ((0, 16),))
    pool = normal_values(part_keys[1], (POOL, D), 1.0, 6.0, ((0, 16),))
    cand_ids = place_ends(jax.random.randint(part_keys[2], (USERS, CAND_USER), 0, POOL), jax.random.fold_in(part_keys[2], 1), 0, POOL - 1).astype(jnp.int32)
    block_user = draw_block_user(jax.random.fold_in(jax.random.fold_in(splits[8], part), 71), part)
    norm_gain = jnp.clip(1.0 + 0.1 * jax.random.normal(splits[4], (D,), jnp.float32), 0.5, 1.5)
    w_in = normal_values(splits[5], (D, 4 * D), D ** -0.5, 0.1875)
    attn_gain = jnp.clip(1.0 + 0.15 * jax.random.normal(splits[6], (D,), jnp.float32), 0.25, 1.75)
    w_out = normal_values(splits[7], (D, D), D ** -0.5, 0.1875)
    return dict(history=history, pool=pool, cand_ids=cand_ids, block_user=block_user, norm_gain=norm_gain, w_in=w_in, attn_gain=attn_gain, w_out=w_out)


def layer_norm(values, gain_vec):
    average = lax.optimization_barrier(jnp.mean(values, axis=-1, keepdims=True))
    centered = values - average
    spread = lax.optimization_barrier(jnp.mean(centered * centered, axis=-1, keepdims=True))
    return centered * lax.rsqrt(spread + 1e-05) * gain_vec

def project_cache(row_block, norm_gain, w_in):
    model_width = row_block.shape[-1]
    flat_rows = row_block.reshape(-1, model_width).astype(jnp.float32)
    normed = layer_norm(flat_rows, norm_gain).astype(jnp.bfloat16)
    front_proj = jnp.dot(normed, w_in[:, 2 * model_width:], preferred_element_type=jnp.float32)
    return jax.nn.silu(front_proj).astype(jnp.bfloat16)

def score_rows(item_rows, keyval, key_owner, norm_gain, w_in, attn_gain, w_out):
    model_width = item_rows.shape[1]
    head_size = model_width // HEADS
    normed = layer_norm(item_rows.astype(jnp.float32), norm_gain).astype(jnp.bfloat16)
    front_proj = jnp.dot(normed, w_in[:, :2 * model_width], preferred_element_type=jnp.float32)
    gate_up = jax.nn.silu(front_proj[:, :model_width])
    queries = jax.nn.silu(front_proj[:, model_width:]).astype(jnp.bfloat16)
    query_heads = queries.reshape(-1, HEADS, head_size).astype(jnp.float32)
    key_heads = keyval[:, :model_width].reshape(-1, HEADS, head_size).astype(jnp.float32)
    value_heads = keyval[:, model_width:].reshape(-1, HEADS, head_size).astype(jnp.float32)
    scores = jnp.einsum('rhd,khd->hrk', query_heads, key_heads)
    row_user = jnp.repeat(jnp.arange(USERS_DEV, dtype=jnp.int32), CAND_USER)
    same_user = row_user[:, None] == key_owner[None, :]
    weights = jnp.where(same_user[None], jax.nn.silu(scores * head_size ** (-0.5)), 0.0).astype(jnp.bfloat16)
    attended = jnp.einsum('hrk,khd->rhd', weights.astype(jnp.float32), value_heads).reshape(-1, model_width)
    gated_rows = (layer_norm(attended, attn_gain) * gate_up).astype(jnp.bfloat16)
    result = jnp.dot(gated_rows, w_out, preferred_element_type=jnp.float32) + item_rows.astype(jnp.float32)
    return result.astype(jnp.bfloat16)

def reference(history, pool, cand_ids, block_user, norm_gain, w_in, attn_gain, w_out):
    dest_flat = (block_user // USERS_DEV).reshape(-1)
    user_flat = block_user.reshape(-1)
    block_order = jnp.arange(BLOCKS, dtype=jnp.int32)
    capacity = N_WIDE * SLOT

    def rank_one(ranker):
        sort_key = jnp.where(dest_flat == ranker, 0, BLOCKS) + block_order
        picked = jnp.argsort(sort_key)[:capacity]
        valid = dest_flat[picked] == ranker
        row_block = jnp.where(valid[:, None, None], history[picked], jnp.zeros((), history.dtype))
        keyval = project_cache(row_block, norm_gain, w_in)
        owner_user = jnp.where(valid, user_flat[picked] - ranker * USERS_DEV, -1)
        key_owner = jnp.repeat(owner_user, BLOCK_ROWS)
        id_rows = lax.dynamic_slice_in_dim(cand_ids, (ranker * USERS_DEV).astype(jnp.int32), USERS_DEV, 0)
        item_rows = jnp.take(pool, id_rows.reshape(-1), axis=0)
        return score_rows(item_rows, keyval, key_owner, norm_gain, w_in, attn_gain, w_out)
    ranked = lax.map(rank_one, jnp.arange(N_WIDE, dtype=jnp.int32))
    return ranked.reshape(USERS, CAND_USER, D)
```

```python
import functools

import jax
import jax.numpy as jnp
from jax import lax
from jax.experimental import pallas as pl
from jax.experimental.pallas import tpu as pltpu
from jax.sharding import PartitionSpec as P

HEADS = 8
GROUPS = 4
F32 = jnp.float32
BF16 = jnp.bfloat16


def silu(x):
    half = 0.5 * x
    return half + half * jnp.tanh(half)


def normalize(values):
    average = jnp.mean(values, axis=-1, keepdims=True)
    centered = values - average
    spread = jnp.mean(centered * centered, axis=-1, keepdims=True)
    return centered * lax.rsqrt(spread + 1e-05)


def flip(me, step, bits):
    total = 0
    for k in range(bits):
        total = total + (1 << k) * lax.rem(me // (1 << k) + step // (1 << k), 2)
    return total


def kernel(
    n, per_user,
    hist_hbm, pool_ref, ids_ref, pos_ref, owner_ref, gain_ref, again_ref, win_hbm, wout_hbm,
    out_ref,
    hist, win, wout, sendb, recvb, poolb, queries, gate, items, normed, acc,
    local_sem, send_sem, recv_sem, pool_send, pool_recv,
):
    bits = (n - 1).bit_length()
    me = lax.axis_index("wide")
    width = hist.shape[1]
    head = width // HEADS
    pair_rows = sendb.shape[1]
    group = n // GROUPS
    rows = group * pair_rows

    local = [
        pltpu.make_async_copy(hist_hbm, hist, local_sem.at[0]),
        pltpu.make_async_copy(win_hbm, win, local_sem.at[1]),
        pltpu.make_async_copy(wout_hbm, wout, local_sem.at[2]),
    ]
    for copy in local:
        copy.start()

    barrier = pltpu.get_barrier_semaphore()

    def greet(step, carry):
        pl.semaphore_signal(
            barrier, inc=1, device_id={"wide": flip(me, step, bits)},
            device_id_type=pl.DeviceIdType.MESH,
        )
        return carry

    lax.fori_loop(1, n, greet, 0)
    poolb[0] = pool_ref[...]

    def block_copy(step):
        return pltpu.make_async_remote_copy(
            src_ref=sendb.at[step], dst_ref=recvb.at[step],
            send_sem=send_sem.at[step], recv_sem=recv_sem.at[step],
            device_id={"wide": flip(me, step, bits)}, device_id_type=pl.DeviceIdType.MESH,
        )

    def pool_copy(stage):
        count = 1 << stage
        return pltpu.make_async_remote_copy(
            src_ref=poolb.at[pl.ds(0, count)], dst_ref=poolb.at[pl.ds(count, count)],
            send_sem=pool_send.at[stage], recv_sem=pool_recv.at[stage],
            device_id={"wide": flip(me, 1 << (bits - 1 - stage), bits)},
            device_id_type=pl.DeviceIdType.MESH,
        )

    def pick(g):
        wanted = lax.broadcasted_iota(jnp.int32, (rows, hist.shape[0]), 0) + g * rows
        chosen = (wanted == pos_ref[...]).astype(F32).astype(BF16)
        found = jnp.dot(chosen, hist[...], preferred_element_type=F32)
        found = found.reshape(group, pair_rows, width).astype(BF16)
        sendb[pl.ds(g * group, group)] = found
        if g == 0:
            recvb[pl.ds(0, 1)] = found[:1]

    def send(g):
        def one(i, carry):
            block_copy((g + 1) * group - 1 - i).start()
            return carry

        lax.fori_loop(0, group if g else group - 1, one, 0)

    local[0].wait()
    pick(GROUPS - 1)
    pl.semaphore_wait(barrier, n - 1)
    pool_copy(0).start()
    for g in reversed(range(GROUPS)):
        send(g)
        if g:
            pick(g - 1)
    for stage in range(bits):
        if stage:
            pool_copy(stage).start()
        pool_copy(stage).wait_recv()

    shards, shard_rows, _ = poolb.shape
    pool_rows = shards * shard_rows
    lanes = lax.broadcasted_iota(jnp.int32, (ids_ref.shape[0], pool_rows), 1)
    chosen = (lanes == ids_ref[...]).astype(F32).astype(BF16)
    table = poolb[...].astype(F32).reshape(pool_rows, width).astype(BF16)
    found = jnp.dot(chosen, table, preferred_element_type=F32)
    items[...] = found.astype(BF16)
    normed_items = (normalize(found) * gain_ref[...]).astype(BF16)
    local[1].wait()
    local[2].wait()
    wide_cols = 2 * head

    def front(j, carry):
        cols = pl.ds(pl.multiple_of(j * wide_cols, wide_cols), wide_cols)
        gate[:, cols] = silu(jnp.dot(normed_items, win[:, cols], preferred_element_type=F32))
        qcols = pl.ds(pl.multiple_of(j * wide_cols + width, wide_cols), wide_cols)
        queries[:, cols] = silu(
            jnp.dot(normed_items, win[:, qcols], preferred_element_type=F32)
        ).astype(BF16)
        return carry

    lax.fori_loop(0, HEADS // 2, front, 0)
    acc[...] = jnp.zeros_like(acc)
    row_user = lax.broadcasted_iota(jnp.int32, (acc.shape[0], rows), 0) // per_user

    for g in range(GROUPS):
        def arrive(step, carry):
            block_copy(step).wait_recv()
            return carry

        lax.fori_loop(max(1, g * group), (g + 1) * group, arrive, 0)
        hidden = recvb[pl.ds(g * group, group)].astype(F32).reshape(rows, width)
        normed[...] = (normalize(hidden) * gain_ref[...]).astype(BF16)
        mask = row_user == owner_ref[:, g * rows:(g + 1) * rows]

        def heads(j, carry):
            cols = pl.ds(pl.multiple_of(j * wide_cols, wide_cols), wide_cols)
            kcols = pl.ds(pl.multiple_of(j * wide_cols + 2 * width, wide_cols), wide_cols)
            vcols = pl.ds(pl.multiple_of(j * wide_cols + 3 * width, wide_cols), wide_cols)
            keys = silu(jnp.dot(normed[...], win[:, kcols], preferred_element_type=F32)).astype(BF16)
            vals = silu(jnp.dot(normed[...], win[:, vcols], preferred_element_type=F32)).astype(BF16)
            query = queries[:, cols]
            parts = []
            for h in range(2):
                part = slice(h * head, (h + 1) * head)
                scores = lax.dot_general(
                    query[:, part], keys[:, part], (((1,), (1,)), ((), ())),
                    preferred_element_type=F32,
                )
                weights = jnp.where(mask, silu(scores * head ** (-0.5)), 0.0).astype(BF16)
                parts.append(jnp.dot(weights, vals[:, part], preferred_element_type=F32))
            acc[:, cols] += jnp.concatenate(parts, axis=1)
            return carry

        lax.fori_loop(0, HEADS // 2, heads, 0)

    gated = (normalize(acc[...]) * again_ref[...] * gate[...]).astype(BF16)

    def last(j, carry):
        cols = pl.ds(pl.multiple_of(j * wide_cols, wide_cols), wide_cols)
        total = jnp.dot(gated, wout[:, cols], preferred_element_type=F32)
        out_ref[:, cols] = (total + items[:, cols].astype(F32)).astype(BF16)
        return carry

    lax.fori_loop(0, HEADS // 2, last, 0)

    for stage in range(bits):
        pool_copy(stage).wait_send()

    def sent(step, carry):
        block_copy(step).wait_send()
        return carry

    lax.fori_loop(1, n, sent, 0)


def body(n, history, pool, cand_ids, block_user, norm_gain, w_in, attn_gain, w_out):
    owned, block_rows, width = history.shape
    users_here, per_user = cand_ids.shape
    slot_count = max(1, 2 * owned // n)
    pair_rows = slot_count * block_rows
    bits = (n - 1).bit_length()
    me = lax.axis_index("wide")

    target = block_user // users_here
    order = jnp.arange(owned, dtype=jnp.int32)
    shared = (target[:, :, None] == target[:, None, :]) & (order[None, None, :] < order[None, :, None])
    within = jnp.sum(shared.astype(jnp.int32), axis=2)
    mine_target = lax.dynamic_index_in_dim(target, me, 0, keepdims=True)
    mine_within = lax.dynamic_index_in_dim(within, me, 0, keepdims=True)
    pos = (mine_target ^ me) * slot_count + mine_within
    pos = (pos[:, :, None] * block_rows + jnp.arange(block_rows, dtype=jnp.int32)).reshape(1, -1)
    owner = jnp.arange(n, dtype=jnp.int32)[:, None] ^ me
    slot = jnp.where(target == me, owner * slot_count + within, -1).reshape(-1, 1)
    label = (block_user - me * users_here + 1).reshape(-1, 1)
    event_slot = jnp.arange(n * pair_rows, dtype=jnp.int32)[None, :] // block_rows
    key_owner = jnp.sum(jnp.where(slot == event_slot, label, 0), axis=0, keepdims=True) - 1

    ids = cand_ids.reshape(-1, 1)
    shard_rows = pool.shape[0]
    relative = (ids // shard_rows) ^ me
    place = jnp.zeros_like(relative)
    for k in range(bits):
        place = place + (((relative >> k) & 1) << (bits - 1 - k))
    ids = place * shard_rows + ids % shard_rows

    cands = users_here * per_user
    vmem = pl.BlockSpec(memory_space=pltpu.VMEM)
    hbm = pl.BlockSpec(memory_space=pl.ANY)
    out = pl.pallas_call(
        functools.partial(kernel, n, per_user),
        out_shape=jax.ShapeDtypeStruct((cands, width), BF16),
        in_specs=[hbm, vmem, vmem, vmem, vmem, vmem, vmem, hbm, hbm],
        out_specs=vmem,
        scratch_shapes=[
            pltpu.VMEM((owned * block_rows, width), BF16),
            pltpu.VMEM(w_in.shape, BF16),
            pltpu.VMEM(w_out.shape, BF16),
            pltpu.VMEM((n, pair_rows, width), BF16),
            pltpu.VMEM((n, pair_rows, width), BF16),
            pltpu.VMEM((n, shard_rows, width), BF16),
            pltpu.VMEM((cands, width), BF16),
            pltpu.VMEM((cands, width), F32),
            pltpu.VMEM((cands, width), BF16),
            pltpu.VMEM((n // GROUPS * pair_rows, width), BF16),
            pltpu.VMEM((cands, width), F32),
            pltpu.SemaphoreType.DMA((3,)),
            pltpu.SemaphoreType.DMA((n,)),
            pltpu.SemaphoreType.DMA((n,)),
            pltpu.SemaphoreType.DMA((bits,)),
            pltpu.SemaphoreType.DMA((bits,)),
        ],
        compiler_params=pltpu.CompilerParams(
            collective_id=0, has_side_effects=True, vmem_limit_bytes=50 * 1024 * 1024
        ),
    )(
        history.reshape(-1, width), pool, ids, pos, key_owner, norm_gain.reshape(1, -1),
        attn_gain.reshape(1, -1), w_in, w_out,
    )
    return out.reshape(users_here, per_user, width)


def solution(mesh):
    in_specs = (
        P(("parts", "wide"), None, None),
        P(("parts", "wide"), None),
        P(("parts", "wide"), None),
        P("parts", None),
        P(),
        P(),
        P(),
        P(),
    )
    out_specs = P(("parts", "wide"), None, None)
    return jax.shard_map(
        functools.partial(body, mesh.shape["wide"]), mesh=mesh, in_specs=in_specs,
        out_specs=out_specs, check_vma=False,
    )
```

```python
import functools

import jax
import jax.numpy as jnp
from jax import lax
from jax.experimental import pallas as pl
from jax.experimental.pallas import tpu as pltpu
from jax.sharding import PartitionSpec as P

HEADS = 8
F32 = jnp.float32
BF16 = jnp.bfloat16


def silu(x):
    half = 0.5 * x
    return half + half * jnp.tanh(half)


def normalize(values):
    average = jnp.mean(values, axis=-1, keepdims=True)
    centered = values - average
    spread = jnp.mean(centered * centered, axis=-1, keepdims=True)
    return centered * lax.rsqrt(spread + 1e-05)


def flip(me, step, bits):
    total = 0
    for k in range(bits):
        total = total + (1 << k) * ((me // (1 << k) + step // (1 << k)) % 2)
    return total


def lane(shape):
    return lax.broadcasted_iota(jnp.int32, shape, len(shape) - 1)


def row(shape):
    return lax.broadcasted_iota(jnp.int32, shape, 0)


def exact_dot(a, b):
    return jnp.dot(a, b, preferred_element_type=F32, precision=lax.Precision.HIGHEST)


def kernel(
    n, users_here, per_user, block_rows,
    hist_hbm, pool_hbm, ids_hbm, user_hbm, gain_hbm, again_hbm, win_hbm, wout_hbm,
    out_ref,
    hist, win, wout, gain, again, ids, block_user, sendb, recvb, poolb,
    queries, mate_queries, gate, items, normed, acc, part_out, part_in,
    local_sem, send_sem, recv_sem, pool_send, pool_recv, part_send, part_recv, ids_sem,
):
    bits = (n - 1).bit_length()
    half, quarter = n // 2, n // 4
    me = lax.axis_index("wide")
    middle = (me // half + me // quarter) % 2
    is_middle = middle == 1
    mate = flip(me, half + quarter, bits)
    owned_rows, width = hist.shape
    owned = owned_rows // block_rows
    head = width // HEADS
    wide_cols = 2 * head
    pair_rows = sendb.shape[1]
    slots = pair_rows // block_rows
    cands = acc.shape[0]
    mesh_id = pl.DeviceIdType.MESH

    sources = (user_hbm, hist_hbm, pool_hbm, ids_hbm, gain_hbm, again_hbm, win_hbm, wout_hbm)
    places = (block_user, hist, poolb.at[0], ids.at[0], gain, again, win, wout)
    local = [
        pltpu.make_async_copy(source, place, local_sem.at[i])
        for i, (source, place) in enumerate(zip(sources, places))
    ]
    for copy in local:
        copy.start()

    barrier = pltpu.get_barrier_semaphore()

    def greet(step, carry):
        pl.semaphore_signal(
            barrier, inc=1, device_id={"wide": flip(me, step, bits)}, device_id_type=mesh_id
        )
        return carry

    lax.fori_loop(1, n, greet, 0)

    def block_copy(step, peer, slot):
        return pltpu.make_async_remote_copy(
            src_ref=sendb.at[step], dst_ref=recvb.at[slot],
            send_sem=send_sem.at[step], recv_sem=recv_sem.at[slot],
            device_id={"wide": flip(me, peer, bits)}, device_id_type=mesh_id,
        )

    def pool_copy(stage):
        count = 1 << stage
        return pltpu.make_async_remote_copy(
            src_ref=poolb.at[pl.ds(0, count)], dst_ref=poolb.at[pl.ds(count, count)],
            send_sem=pool_send.at[stage], recv_sem=pool_recv.at[stage],
            device_id={"wide": flip(me, 1 << (bits - 1 - stage), bits)}, device_id_type=mesh_id,
        )

    ids_copy = pltpu.make_async_remote_copy(
        src_ref=ids.at[0], dst_ref=ids.at[1], send_sem=ids_sem.at[0], recv_sem=ids_sem.at[1],
        device_id={"wide": mate}, device_id_type=mesh_id,
    )

    def part_copy(j):
        return pltpu.make_async_remote_copy(
            src_ref=part_out.at[j], dst_ref=part_in.at[j],
            send_sem=part_send.at[j], recv_sem=part_recv.at[j],
            device_id={"wide": mate}, device_id_type=mesh_id,
        )

    local[0].wait()
    users = block_user[...]
    targets = users // users_here
    mine = jnp.sum(jnp.where(row((n, owned)) == me, targets, 0), axis=0, keepdims=True)
    square = (owned, owned)
    mine_down = jnp.sum(jnp.where(row(square) == lane(square), mine, 0), axis=1, keepdims=True)
    earlier = row(square) < lane(square)
    within = jnp.sum(
        jnp.where((mine_down == mine) & earlier, 1, 0), axis=0, keepdims=True
    )
    position = flip(me, mine, bits) * slots + within
    spread_shape = (owned, owned_rows)
    spread = jnp.where(lane(spread_shape) // block_rows == row(spread_shape), 1.0, 0.0)
    position = exact_dot(jnp.broadcast_to(position.astype(F32), (8, owned)), spread)[:1]
    position = position.astype(jnp.int32) * block_rows + lane((1, owned_rows)) % block_rows
    for copy in local[1:4]:
        copy.wait()

    def pick(first, count):
        wanted = row((count * pair_rows, owned_rows)) + first * pair_rows
        chosen = jnp.where(wanted == position, 1.0, 0.0).astype(BF16)
        found = jnp.dot(chosen, hist[...], preferred_element_type=F32)
        sendb[pl.ds(first, count)] = found.reshape(count, pair_rows, width).astype(BF16)

    def send_all(first, last, peer_shift, slot_shift):
        def one(i, carry):
            step = last - 1 - i
            block_copy(step, step - peer_shift, step + slot_shift).start()
            return carry

        lax.fori_loop(0, last - first, one, 0)

    pl.semaphore_wait(barrier, n - 1)
    pool_copy(0).start()
    ids_copy.start()
    pick(half + quarter, quarter)
    pool_copy(0).wait_recv()
    pool_copy(1).start()
    pick(half, quarter)
    pool_copy(1).wait_recv()
    pool_copy(2).start()

    @pl.when(is_middle)
    def _():
        recvb[pl.ds(half, 1)] = sendb[pl.ds(half + quarter, 1)]
        send_all(half + quarter + 1, n, half + quarter, -quarter)
        send_all(half, half + quarter, 0, 0)

    @pl.when(jnp.logical_not(is_middle))
    def _():
        send_all(half, half + quarter, quarter, quarter)
        send_all(half + quarter, n, 0, 0)

    pick(quarter, quarter)
    for stage in range(3, bits):
        pool_copy(stage - 1).wait_recv()
        pool_copy(stage).start()
    pick(0, quarter)
    send_all(1, half, 0, 0)
    recvb[pl.ds(0, 1)] = sendb[pl.ds(0, 1)]
    pool_copy(bits - 1).wait_recv()

    def event_users(ranker, first, flips_from):
        shape = (n, half * pair_rows)
        arrived = targets == ranker
        count = exact_dot(jnp.where(arrived, 1.0, 0.0), jnp.where(earlier, 1.0, 0.0))
        count = count.astype(jnp.int32)
        label = users - ranker * users_here + 1
        lanes = lane(shape)
        slot_here = (lanes % pair_rows) // block_rows
        owner = flip(me, lane((1, half * pair_rows)) // pair_rows + flips_from, bits)
        total = jnp.zeros(shape, jnp.int32)
        for slot in range(slots):
            at_slot = jnp.sum(
                jnp.where(arrived & (count == slot), label, 0), axis=1, keepdims=True
            )
            total = total + jnp.where(slot_here == slot, at_slot, 0)
        return jnp.sum(jnp.where(row(shape) == owner, total, 0), axis=0, keepdims=True) - 1

    near_users = event_users(me, 0, 0)
    far_users = event_users(jnp.where(is_middle, mate, me), half, half * (1 - middle))

    shards, shard_rows, _ = poolb.shape
    pool_rows = shards * shard_rows
    for copy in local[4:]:
        copy.wait()

    def pool_items(which):
        wanted = ids[which]
        relative = flip(me, wanted // shard_rows, bits)
        place = jnp.zeros_like(relative)
        for k in range(bits):
            place = place + ((relative // (1 << k)) % 2) * (1 << (bits - 1 - k))
        place = place * shard_rows + wanted % shard_rows
        table = poolb[...].astype(F32).reshape(pool_rows, width).astype(BF16)
        found = []
        for u in range(users_here):
            chosen = jnp.where(row((pool_rows, per_user)) == place[u:u + 1], 1.0, 0.0).astype(BF16)
            found.append(lax.dot_general(
                chosen, table, (((0,), (0,)), ((), ())), preferred_element_type=F32
            ))
        found = jnp.concatenate(found, axis=0)
        return found, (normalize(found) * gain[...]).astype(BF16)

    def columns(j, offset=0):
        return pl.ds(pl.multiple_of(j * wide_cols + offset, wide_cols), wide_cols)

    def project(rows_in, j, offset):
        return silu(jnp.dot(rows_in, win[:, columns(j, offset)], preferred_element_type=F32))

    def each_pair(step):
        def one(j, carry):
            step(j)
            return carry

        lax.fori_loop(0, HEADS // 2, one, 0)

    def attend(first, count, query_ref, event_user, emit):
        rows = count * pair_rows
        hidden = recvb[pl.ds(first, count)].astype(F32).reshape(rows, width)
        normed[pl.ds(0, rows)] = (normalize(hidden) * gain[...]).astype(BF16)
        mask = row((cands, rows)) // per_user == event_user

        def pair(j):
            here = normed[pl.ds(0, rows)]
            keys = project(here, j, 2 * width).astype(BF16)
            vals = project(here, j, 3 * width).astype(BF16)
            query = query_ref[:, columns(j)]
            parts = []
            for h in range(2):
                part = slice(h * head, (h + 1) * head)
                scores = lax.dot_general(
                    query[:, part], keys[:, part], (((1,), (1,)), ((), ())),
                    preferred_element_type=F32,
                )
                weights = jnp.where(mask, silu(scores * head ** (-0.5)), 0.0).astype(BF16)
                parts.append(jnp.dot(weights, vals[:, part], preferred_element_type=F32))
            emit(j, jnp.concatenate(parts, axis=1))

        each_pair(pair)

    def arrive(first, last):
        def one(slot, carry):
            block_copy(slot, slot, slot).wait_recv()
            return carry

        lax.fori_loop(first, last, one, 0)

    def add(j, value):
        acc[:, columns(j)] += value

    ids_copy.wait_recv()

    @pl.when(is_middle)
    def _():
        _, mate_items = pool_items(1)

        def ask(j):
            mate_queries[:, columns(j)] = project(mate_items, j, width).astype(BF16)

        each_pair(ask)
        arrive(half + 1, n)

        def emit(j, value):
            part_out[j] = value.astype(BF16)
            part_copy(j).start()

        attend(half, half, mate_queries, far_users, emit)

    found, normed_items = pool_items(0)
    items[...] = found.astype(BF16)

    def front(j):
        gate[:, columns(j)] = project(normed_items, j, 0)
        queries[:, columns(j)] = project(normed_items, j, width).astype(BF16)

    each_pair(front)
    acc[...] = jnp.zeros_like(acc)
    arrive(1, half)
    attend(0, half, queries, near_users, add)

    @pl.when(is_middle)
    def _():
        def join(j):
            part_copy(j).wait_recv()
            add(j, part_in[j].astype(F32))

        each_pair(join)

    @pl.when(jnp.logical_not(is_middle))
    def _():
        for g in range(2):
            first = half + g * quarter
            arrive(first, first + quarter)
            event_user = far_users[:, g * quarter * pair_rows:(g + 1) * quarter * pair_rows]
            attend(first, quarter, queries, event_user, add)

    gated = (normalize(acc[...]) * again[...] * gate[...]).astype(BF16)

    def last(j):
        total = jnp.dot(gated, wout[:, columns(j)], preferred_element_type=F32)
        out_ref[:, columns(j)] = (total + items[:, columns(j)].astype(F32)).astype(BF16)

    each_pair(last)

    ids_copy.wait_send()
    for stage in range(bits):
        pool_copy(stage).wait_send()

    def sent(step, carry):
        block_copy(step, 1, step).wait_send()
        return carry

    lax.fori_loop(1, half + quarter, sent, 0)
    lax.fori_loop(half + quarter + 1, n, sent, 0)

    @pl.when(jnp.logical_not(is_middle))
    def _():
        sent(half + quarter, 0)

    @pl.when(is_middle)
    def _():
        each_pair(lambda j: part_copy(j).wait_send())


def body(n, history, pool, cand_ids, block_user, norm_gain, w_in, attn_gain, w_out):
    owned, block_rows, width = history.shape
    users_here, per_user = cand_ids.shape
    slot_count = max(1, 2 * owned // n)
    pair_rows = slot_count * block_rows
    shard_rows = pool.shape[0]
    bits = (n - 1).bit_length()
    cands = users_here * per_user
    pairs = (HEADS // 2, cands, 2 * width // HEADS)
    hbm = pl.BlockSpec(memory_space=pl.ANY)
    dma = pltpu.SemaphoreType.DMA
    out = pl.pallas_call(
        functools.partial(kernel, n, users_here, per_user, block_rows),
        out_shape=jax.ShapeDtypeStruct((cands, width), BF16),
        in_specs=[hbm] * 8,
        out_specs=pl.BlockSpec(memory_space=pltpu.VMEM),
        scratch_shapes=[
            pltpu.VMEM((owned * block_rows, width), BF16),
            pltpu.VMEM(w_in.shape, BF16),
            pltpu.VMEM(w_out.shape, BF16),
            pltpu.VMEM((1, width), F32),
            pltpu.VMEM((1, width), F32),
            pltpu.VMEM((2,) + cand_ids.shape, jnp.int32),
            pltpu.VMEM(block_user.shape, jnp.int32),
            pltpu.VMEM((n, pair_rows, width), BF16),
            pltpu.VMEM((n, pair_rows, width), BF16),
            pltpu.VMEM((n, shard_rows, width), BF16),
            pltpu.VMEM((cands, width), BF16),
            pltpu.VMEM((cands, width), BF16),
            pltpu.VMEM((cands, width), F32),
            pltpu.VMEM((cands, width), BF16),
            pltpu.VMEM((n // 2 * pair_rows, width), BF16),
            pltpu.VMEM((cands, width), F32),
            pltpu.VMEM(pairs, BF16),
            pltpu.VMEM(pairs, BF16),
            dma((8,)),
            dma((n,)),
            dma((n,)),
            dma((bits,)),
            dma((bits,)),
            dma((HEADS // 2,)),
            dma((HEADS // 2,)),
            dma((2,)),
        ],
        compiler_params=pltpu.CompilerParams(
            collective_id=0, has_side_effects=True, vmem_limit_bytes=56 * 1024 * 1024
        ),
    )(
        history.reshape(-1, width), pool, cand_ids, block_user, norm_gain.reshape(1, -1),
        attn_gain.reshape(1, -1), w_in, w_out,
    )
    return out.reshape(users_here, per_user, width)


def solution(mesh):
    in_specs = (
        P(("parts", "wide"), None, None),
        P(("parts", "wide"), None),
        P(("parts", "wide"), None),
        P("parts", None),
        P(),
        P(),
        P(),
        P(),
    )
    out_specs = P(("parts", "wide"), None, None)
    return jax.shard_map(
        functools.partial(body, mesh.shape["wide"]), mesh=mesh, in_specs=in_specs,
        out_specs=out_specs, check_vma=False,
    )
```

```python
import functools

import jax
import jax.numpy as jnp
from jax import lax
from jax.experimental import pallas as pl
from jax.experimental.pallas import tpu as pltpu
from jax.sharding import PartitionSpec as P

HEADS = 8
F32 = jnp.float32
BF16 = jnp.bfloat16


def silu(x):
    half = 0.5 * x
    return half + half * jnp.tanh(half)


def normalize(values):
    average = jnp.mean(values, axis=-1, keepdims=True)
    centered = values - average
    spread = jnp.mean(centered * centered, axis=-1, keepdims=True)
    return centered * lax.rsqrt(spread + 1e-05)


def flip(me, step, bits):
    total = 0
    for k in range(bits):
        total = total + (1 << k) * ((me // (1 << k) + step // (1 << k)) % 2)
    return total


def lane(shape):
    return lax.broadcasted_iota(jnp.int32, shape, len(shape) - 1)


def row(shape):
    return lax.broadcasted_iota(jnp.int32, shape, 0)


def exact_dot(a, b):
    return jnp.dot(a, b, preferred_element_type=F32, precision=lax.Precision.HIGHEST)


def kernel(
    n, users_here, per_user, block_rows,
    hist_hbm, pool_hbm, ids_hbm, user_hbm, gain_hbm, again_hbm, win_hbm, wout_hbm,
    out_ref,
    hist, win, wout, gain, again, ids, block_user, sendb, recvb, poolb,
    queries, mate_queries, gate, items, normed, acc, part_out, part_in,
    local_sem, send_sem, recv_sem, pool_send, pool_recv, part_send, part_recv, ids_sem,
):
    bits = (n - 1).bit_length()
    half, quarter = n // 2, n // 4
    me = lax.axis_index("wide")
    middle = (me // half + me // quarter) % 2
    is_middle = middle == 1
    mate = flip(me, half + quarter, bits)
    owned_rows, width = hist.shape
    owned = owned_rows // block_rows
    head = width // HEADS
    wide_cols = 2 * head
    pair_rows = sendb.shape[1]
    slots = pair_rows // block_rows
    cands = acc.shape[0]
    mesh_id = pl.DeviceIdType.MESH

    sources = (user_hbm, hist_hbm, pool_hbm, ids_hbm, gain_hbm, again_hbm, win_hbm, wout_hbm)
    places = (block_user, hist, poolb.at[0], ids.at[0], gain, again, win, wout)
    local = [
        pltpu.make_async_copy(source, place, local_sem.at[i])
        for i, (source, place) in enumerate(zip(sources, places))
    ]
    for copy in local:
        copy.start()

    barrier = pltpu.get_barrier_semaphore()

    def greet(step, carry):
        pl.semaphore_signal(
            barrier, inc=1, device_id={"wide": flip(me, step, bits)}, device_id_type=mesh_id
        )
        return carry

    lax.fori_loop(1, n, greet, 0)

    def block_copy(step, peer, slot):
        return pltpu.make_async_remote_copy(
            src_ref=sendb.at[step], dst_ref=recvb.at[slot],
            send_sem=send_sem.at[step], recv_sem=recv_sem.at[slot],
            device_id={"wide": flip(me, peer, bits)}, device_id_type=mesh_id,
        )

    def pool_copy(stage):
        count = 1 << stage
        return pltpu.make_async_remote_copy(
            src_ref=poolb.at[pl.ds(0, count)], dst_ref=poolb.at[pl.ds(count, count)],
            send_sem=pool_send.at[stage], recv_sem=pool_recv.at[stage],
            device_id={"wide": flip(me, 1 << (bits - 1 - stage), bits)}, device_id_type=mesh_id,
        )

    ids_copy = pltpu.make_async_remote_copy(
        src_ref=ids.at[0], dst_ref=ids.at[1], send_sem=ids_sem.at[0], recv_sem=ids_sem.at[1],
        device_id={"wide": mate}, device_id_type=mesh_id,
    )

    def part_copy(j):
        return pltpu.make_async_remote_copy(
            src_ref=part_out.at[j], dst_ref=part_in.at[j],
            send_sem=part_send.at[j], recv_sem=part_recv.at[j],
            device_id={"wide": mate}, device_id_type=mesh_id,
        )

    local[0].wait()
    users = block_user[...]
    targets = users // users_here
    mine = jnp.sum(jnp.where(row((n, owned)) == me, targets, 0), axis=0, keepdims=True)
    square = (owned, owned)
    mine_down = jnp.sum(jnp.where(row(square) == lane(square), mine, 0), axis=1, keepdims=True)
    earlier = row(square) < lane(square)
    within = jnp.sum(
        jnp.where((mine_down == mine) & earlier, 1, 0), axis=0, keepdims=True
    )
    position = flip(me, mine, bits) * slots + within
    spread_shape = (owned, owned_rows)
    spread = jnp.where(lane(spread_shape) // block_rows == row(spread_shape), 1.0, 0.0)
    position = exact_dot(jnp.broadcast_to(position.astype(F32), (8, owned)), spread)[:1]
    position = position.astype(jnp.int32) * block_rows + lane((1, owned_rows)) % block_rows
    for copy in local[1:4]:
        copy.wait()

    def pick(first, count):
        wanted = row((count * pair_rows, owned_rows)) + first * pair_rows
        chosen = jnp.where(wanted == position, 1.0, 0.0).astype(BF16)
        found = jnp.dot(chosen, hist[...], preferred_element_type=F32)
        sendb[pl.ds(first, count)] = found.reshape(count, pair_rows, width).astype(BF16)

    def send(step, peer_shift, slot_shift):
        block_copy(step, step - peer_shift, step + slot_shift).start()

    pick(half, quarter)
    pick(half + quarter, quarter)
    pl.semaphore_wait(barrier, n - 1)
    pool_copy(0).start()
    ids_copy.start()
    pick(quarter, quarter)
    pool_copy(0).wait_recv()
    pool_copy(1).start()

    @pl.when(is_middle)
    def _():
        recvb[pl.ds(half, 1)] = sendb[pl.ds(half + quarter, 1)]

        def one(i, carry):
            send(half + i, 0, 0)
            send(quarter + i, 0, 0)
            return carry

        def proxied(i, carry):
            send(half + quarter + i, half + quarter, -quarter)
            return carry

        lax.fori_loop(1, quarter, proxied, 0)
        lax.fori_loop(0, quarter, one, 0)

    @pl.when(jnp.logical_not(is_middle))
    def _():
        def one(i, carry):
            send(half + i, quarter, quarter)
            send(half + quarter + i, 0, 0)
            return carry

        def near(i, carry):
            send(quarter + i, 0, 0)
            return carry

        lax.fori_loop(0, quarter, one, 0)
        lax.fori_loop(0, quarter, near, 0)

    pick(0, quarter)
    recvb[pl.ds(0, 1)] = sendb[pl.ds(0, 1)]
    for stage in range(2, bits):
        pool_copy(stage - 1).wait_recv()
        pool_copy(stage).start()

    def plane(i, carry):
        send(i, 0, 0)
        return carry

    lax.fori_loop(1, quarter, plane, 0)
    pool_copy(bits - 1).wait_recv()

    def event_users(ranker, first, flips_from):
        shape = (n, half * pair_rows)
        arrived = targets == ranker
        count = exact_dot(jnp.where(arrived, 1.0, 0.0), jnp.where(earlier, 1.0, 0.0))
        count = count.astype(jnp.int32)
        label = users - ranker * users_here + 1
        lanes = lane(shape)
        slot_here = (lanes % pair_rows) // block_rows
        owner = flip(me, lane((1, half * pair_rows)) // pair_rows + flips_from, bits)
        total = jnp.zeros(shape, jnp.int32)
        for slot in range(slots):
            at_slot = jnp.sum(
                jnp.where(arrived & (count == slot), label, 0), axis=1, keepdims=True
            )
            total = total + jnp.where(slot_here == slot, at_slot, 0)
        return jnp.sum(jnp.where(row(shape) == owner, total, 0), axis=0, keepdims=True) - 1

    near_users = event_users(me, 0, 0)
    far_users = event_users(jnp.where(is_middle, mate, me), half, half * (1 - middle))

    shards, shard_rows, _ = poolb.shape
    pool_rows = shards * shard_rows
    for copy in local[4:]:
        copy.wait()

    def pool_items(which):
        wanted = ids[which]
        relative = flip(me, wanted // shard_rows, bits)
        place = jnp.zeros_like(relative)
        for k in range(bits):
            place = place + ((relative // (1 << k)) % 2) * (1 << (bits - 1 - k))
        place = place * shard_rows + wanted % shard_rows
        table = poolb[...].astype(F32).reshape(pool_rows, width).astype(BF16)
        found = []
        for u in range(users_here):
            chosen = jnp.where(row((pool_rows, per_user)) == place[u:u + 1], 1.0, 0.0).astype(BF16)
            found.append(lax.dot_general(
                chosen, table, (((0,), (0,)), ((), ())), preferred_element_type=F32
            ))
        found = jnp.concatenate(found, axis=0)
        return found, (normalize(found) * gain[...]).astype(BF16)

    def columns(j, offset=0):
        return pl.ds(pl.multiple_of(j * wide_cols + offset, wide_cols), wide_cols)

    def project(rows_in, j, offset):
        return silu(jnp.dot(rows_in, win[:, columns(j, offset)], preferred_element_type=F32))

    def each_pair(step):
        def one(j, carry):
            step(j)
            return carry

        lax.fori_loop(0, HEADS // 2, one, 0)

    def attend(first, count, query_ref, event_user, emit):
        rows = count * pair_rows
        hidden = recvb[pl.ds(first, count)].astype(F32).reshape(rows, width)
        normed[pl.ds(0, rows)] = (normalize(hidden) * gain[...]).astype(BF16)
        mask = row((cands, rows)) // per_user == event_user

        def pair(j):
            here = normed[pl.ds(0, rows)]
            keys = project(here, j, 2 * width).astype(BF16)
            vals = project(here, j, 3 * width).astype(BF16)
            query = query_ref[:, columns(j)]
            parts = []
            for h in range(2):
                part = slice(h * head, (h + 1) * head)
                scores = lax.dot_general(
                    query[:, part], keys[:, part], (((1,), (1,)), ((), ())),
                    preferred_element_type=F32,
                )
                weights = jnp.where(mask, silu(scores * head ** (-0.5)), 0.0).astype(BF16)
                parts.append(jnp.dot(weights, vals[:, part], preferred_element_type=F32))
            emit(j, jnp.concatenate(parts, axis=1))

        each_pair(pair)

    def arrive(first, last):
        def one(slot, carry):
            block_copy(slot, slot, slot).wait_recv()
            return carry

        lax.fori_loop(first, last, one, 0)

    def add(j, value):
        acc[:, columns(j)] += value

    ids_copy.wait_recv()

    @pl.when(is_middle)
    def _():
        _, mate_items = pool_items(1)

        def ask(j):
            mate_queries[:, columns(j)] = project(mate_items, j, width).astype(BF16)

        each_pair(ask)
        arrive(half + 1, n)

        def emit(j, value):
            part_out[j] = value.astype(BF16)
            part_copy(j).start()

        attend(half, half, mate_queries, far_users, emit)

    found, normed_items = pool_items(0)
    items[...] = found.astype(BF16)

    def front(j):
        gate[:, columns(j)] = project(normed_items, j, 0)
        queries[:, columns(j)] = project(normed_items, j, width).astype(BF16)

    each_pair(front)
    acc[...] = jnp.zeros_like(acc)
    arrive(1, half)
    attend(0, half, queries, near_users, add)

    @pl.when(is_middle)
    def _():
        def join(j):
            part_copy(j).wait_recv()
            add(j, part_in[j].astype(F32))

        each_pair(join)

    @pl.when(jnp.logical_not(is_middle))
    def _():
        for g in range(2):
            first = half + g * quarter
            arrive(first, first + quarter)
            event_user = far_users[:, g * quarter * pair_rows:(g + 1) * quarter * pair_rows]
            attend(first, quarter, queries, event_user, add)

    gated = (normalize(acc[...]) * again[...] * gate[...]).astype(BF16)

    def last(j):
        total = jnp.dot(gated, wout[:, columns(j)], preferred_element_type=F32)
        out_ref[:, columns(j)] = (total + items[:, columns(j)].astype(F32)).astype(BF16)

    each_pair(last)

    ids_copy.wait_send()
    for stage in range(bits):
        pool_copy(stage).wait_send()

    def sent(step, carry):
        block_copy(step, 1, step).wait_send()
        return carry

    lax.fori_loop(1, half + quarter, sent, 0)
    lax.fori_loop(half + quarter + 1, n, sent, 0)

    @pl.when(jnp.logical_not(is_middle))
    def _():
        sent(half + quarter, 0)

    @pl.when(is_middle)
    def _():
        each_pair(lambda j: part_copy(j).wait_send())


def body(n, history, pool, cand_ids, block_user, norm_gain, w_in, attn_gain, w_out):
    owned, block_rows, width = history.shape
    users_here, per_user = cand_ids.shape
    slot_count = max(1, 2 * owned // n)
    pair_rows = slot_count * block_rows
    shard_rows = pool.shape[0]
    bits = (n - 1).bit_length()
    cands = users_here * per_user
    pairs = (HEADS // 2, cands, 2 * width // HEADS)
    hbm = pl.BlockSpec(memory_space=pl.ANY)
    dma = pltpu.SemaphoreType.DMA
    out = pl.pallas_call(
        functools.partial(kernel, n, users_here, per_user, block_rows),
        out_shape=jax.ShapeDtypeStruct((cands, width), BF16),
        in_specs=[hbm] * 8,
        out_specs=pl.BlockSpec(memory_space=pltpu.VMEM),
        scratch_shapes=[
            pltpu.VMEM((owned * block_rows, width), BF16),
            pltpu.VMEM(w_in.shape, BF16),
            pltpu.VMEM(w_out.shape, BF16),
            pltpu.VMEM((1, width), F32),
            pltpu.VMEM((1, width), F32),
            pltpu.VMEM((2,) + cand_ids.shape, jnp.int32),
            pltpu.VMEM(block_user.shape, jnp.int32),
            pltpu.VMEM((n, pair_rows, width), BF16),
            pltpu.VMEM((n, pair_rows, width), BF16),
            pltpu.VMEM((n, shard_rows, width), BF16),
            pltpu.VMEM((cands, width), BF16),
            pltpu.VMEM((cands, width), BF16),
            pltpu.VMEM((cands, width), F32),
            pltpu.VMEM((cands, width), BF16),
            pltpu.VMEM((n // 2 * pair_rows, width), BF16),
            pltpu.VMEM((cands, width), F32),
            pltpu.VMEM(pairs, BF16),
            pltpu.VMEM(pairs, BF16),
            dma((8,)),
            dma((n,)),
            dma((n,)),
            dma((bits,)),
            dma((bits,)),
            dma((HEADS // 2,)),
            dma((HEADS // 2,)),
            dma((2,)),
        ],
        compiler_params=pltpu.CompilerParams(
            collective_id=0, has_side_effects=True, vmem_limit_bytes=40 * 1024 * 1024
        ),
    )(
        history.reshape(-1, width), pool, cand_ids, block_user, norm_gain.reshape(1, -1),
        attn_gain.reshape(1, -1), w_in, w_out,
    )
    return out.reshape(users_here, per_user, width)


def solution(mesh):
    in_specs = (
        P(("parts", "wide"), None, None),
        P(("parts", "wide"), None),
        P(("parts", "wide"), None),
        P("parts", None),
        P(),
        P(),
        P(),
        P(),
    )
    out_specs = P(("parts", "wide"), None, None)
    return jax.shard_map(
        functools.partial(body, mesh.shape["wide"]), mesh=mesh, in_specs=in_specs,
        out_specs=out_specs, check_vma=False,
    )
```

```python
import functools

import jax
import jax.numpy as jnp
from jax import lax
from jax.experimental import pallas as pl
from jax.experimental.pallas import tpu as pltpu
from jax.sharding import PartitionSpec as P

HEADS = 8
STEPS = 4
F32 = jnp.float32
BF16 = jnp.bfloat16


def silu(x):
    half = 0.5 * x
    return half + half * jnp.tanh(half)


def normalize(values):
    average = jnp.mean(values, axis=-1, keepdims=True)
    centered = values - average
    spread = jnp.mean(centered * centered, axis=-1, keepdims=True)
    return centered * lax.rsqrt(spread + 1e-05)


def flip(me, step, bits):
    total = 0
    for k in range(bits):
        total = total + (1 << k) * ((me // (1 << k) + step // (1 << k)) % 2)
    return total


def lane(shape):
    return lax.broadcasted_iota(jnp.int32, shape, len(shape) - 1)


def row(shape):
    return lax.broadcasted_iota(jnp.int32, shape, 0)


def exact_dot(a, b):
    return jnp.dot(a, b, preferred_element_type=F32, precision=lax.Precision.HIGHEST)


def kernel(
    n, users_here, per_user, block_rows,
    hist_hbm, pool_hbm, ids_hbm, user_hbm, gain_hbm, again_hbm, win_hbm, wout_hbm,
    out_ref,
    hist, win, wout, gain, again, ids, block_user, sendb, recvb, poolb,
    queries, mate_queries, gate, items, normed, acc, part_out, part_in,
    local_sem, send_sem, recv_sem, pool_send, pool_recv, part_send, part_recv, ids_sem,
):
    bits = (n - 1).bit_length()
    half, quarter = n // 2, n // 4
    unit = quarter // STEPS
    me = lax.axis_index("wide")
    middle = (me // half + me // quarter) % 2
    is_middle = middle == 1
    mate = flip(me, half + quarter, bits)
    owned_rows, width = hist.shape
    owned = owned_rows // block_rows
    head = width // HEADS
    wide_cols = 2 * head
    pair_rows = sendb.shape[1]
    slots = pair_rows // block_rows
    cands = acc.shape[0]
    mesh_id = pl.DeviceIdType.MESH

    sources = (user_hbm, hist_hbm, pool_hbm, ids_hbm, gain_hbm, again_hbm, win_hbm, wout_hbm)
    places = (block_user, hist, poolb.at[0], ids.at[0], gain, again, win, wout)
    local = [
        pltpu.make_async_copy(source, place, local_sem.at[i])
        for i, (source, place) in enumerate(zip(sources, places))
    ]
    for copy in local:
        copy.start()

    barrier = pltpu.get_barrier_semaphore()

    def greet(step, carry):
        pl.semaphore_signal(
            barrier, inc=1, device_id={"wide": flip(me, step, bits)}, device_id_type=mesh_id
        )
        return carry

    lax.fori_loop(1, n, greet, 0)

    def block_copy(step, peer, slot):
        return pltpu.make_async_remote_copy(
            src_ref=sendb.at[step], dst_ref=recvb.at[slot],
            send_sem=send_sem.at[step], recv_sem=recv_sem.at[slot],
            device_id={"wide": flip(me, peer, bits)}, device_id_type=mesh_id,
        )

    def pool_copy(stage):
        count = 1 << stage
        return pltpu.make_async_remote_copy(
            src_ref=poolb.at[pl.ds(0, count)], dst_ref=poolb.at[pl.ds(count, count)],
            send_sem=pool_send.at[stage], recv_sem=pool_recv.at[stage],
            device_id={"wide": flip(me, 1 << (bits - 1 - stage), bits)}, device_id_type=mesh_id,
        )

    ids_copy = pltpu.make_async_remote_copy(
        src_ref=ids.at[0], dst_ref=ids.at[1], send_sem=ids_sem.at[0], recv_sem=ids_sem.at[1],
        device_id={"wide": mate}, device_id_type=mesh_id,
    )

    def part_copy(j):
        return pltpu.make_async_remote_copy(
            src_ref=part_out.at[j], dst_ref=part_in.at[j],
            send_sem=part_send.at[j], recv_sem=part_recv.at[j],
            device_id={"wide": mate}, device_id_type=mesh_id,
        )

    local[0].wait()
    users = block_user[...]
    targets = users // users_here
    mine = jnp.sum(jnp.where(row((n, owned)) == me, targets, 0), axis=0, keepdims=True)
    square = (owned, owned)
    mine_down = jnp.sum(jnp.where(row(square) == lane(square), mine, 0), axis=1, keepdims=True)
    earlier = row(square) < lane(square)
    within = jnp.sum(
        jnp.where((mine_down == mine) & earlier, 1, 0), axis=0, keepdims=True
    )
    position = flip(me, mine, bits) * slots + within
    spread_shape = (owned, owned_rows)
    spread = jnp.where(lane(spread_shape) // block_rows == row(spread_shape), 1.0, 0.0)
    position = exact_dot(jnp.broadcast_to(position.astype(F32), (8, owned)), spread)[:1]
    position = position.astype(jnp.int32) * block_rows + lane((1, owned_rows)) % block_rows
    for copy in local[1:4]:
        copy.wait()

    def pick(first, count):
        wanted = row((count * pair_rows, owned_rows)) + first * pair_rows
        chosen = jnp.where(wanted == position, 1.0, 0.0).astype(BF16)
        found = jnp.dot(chosen, hist[...], preferred_element_type=F32)
        sendb[pl.ds(first, count)] = found.reshape(count, pair_rows, width).astype(BF16)

    def run(act, first, count, peer_shift=0, slot_shift=0):
        def one(i, carry):
            copy = block_copy(first + i, first + i - peer_shift, first + i + slot_shift)
            copy.start() if act else copy.wait_send()
            return carry

        lax.fori_loop(0, count, one, 0)

    def end_step(i, act):
        if i < STEPS // 2:
            run(act, half + 2 * i * unit, 2 * unit, quarter, quarter)
        run(act, half + quarter + i * unit, unit)
        if i >= STEPS // 2:
            run(act, quarter + (2 * i - STEPS) * unit, 2 * unit)

    def middle_step(i, act):
        run(act, half + i * unit, unit)
        run(act, quarter + i * unit, unit)

    def turn(step, i):
        step(i - 1, False)
        step(i, True)

    pick(half, quarter)
    pick(half + quarter, quarter)
    pl.semaphore_wait(barrier, n - 1)
    pool_copy(0).start()
    ids_copy.start()
    pick(quarter, quarter)
    pool_copy(0).wait_recv()
    pool_copy(1).start()

    @pl.when(is_middle)
    def _():
        recvb[pl.ds(half, 1)] = sendb[pl.ds(half + quarter, 1)]

        run(True, half + quarter + 1, quarter - 1, half + quarter, -quarter)
        middle_step(0, True)

    @pl.when(jnp.logical_not(is_middle))
    def _():
        end_step(0, True)

    pick(0, quarter)
    recvb[pl.ds(0, 1)] = sendb[pl.ds(0, 1)]
    for stage in range(2, bits):
        pool_copy(stage - 1).wait_recv()
        pool_copy(stage).start()

    run(True, 1, quarter - 1)
    pool_copy(bits - 1).wait_recv()

    def by_slot(ranker):
        arrived = targets == ranker
        count = exact_dot(jnp.where(arrived, 1.0, 0.0), jnp.where(earlier, 1.0, 0.0))
        count = count.astype(jnp.int32)
        label = users - ranker * users_here + 1
        return [
            jnp.sum(jnp.where(arrived & (count == slot), label, 0), axis=1, keepdims=True)
            for slot in range(slots)
        ]

    def by_event(table, blocks, step_of):
        shape = (n, blocks * pair_rows)
        slot_here = (lane(shape) % pair_rows) // block_rows
        owner = flip(me, step_of(lane((1, shape[1])) // pair_rows), bits)
        total = jnp.zeros(shape, jnp.int32)
        for slot in range(slots):
            total = total + jnp.where(slot_here == slot, table[slot], 0)
        return jnp.sum(jnp.where(row(shape) == owner, total, 0), axis=0, keepdims=True) - 1

    own_table = by_slot(me)

    shards, shard_rows, _ = poolb.shape
    pool_rows = shards * shard_rows
    for copy in local[4:]:
        copy.wait()

    def pool_items(which):
        wanted = ids[which]
        relative = flip(me, wanted // shard_rows, bits)
        place = jnp.zeros_like(relative)
        for k in range(bits):
            place = place + ((relative // (1 << k)) % 2) * (1 << (bits - 1 - k))
        place = place * shard_rows + wanted % shard_rows
        table = poolb[...].astype(F32).reshape(pool_rows, width).astype(BF16)
        found = []
        for u in range(users_here):
            chosen = jnp.where(row((pool_rows, per_user)) == place[u:u + 1], 1.0, 0.0).astype(BF16)
            found.append(lax.dot_general(
                chosen, table, (((0,), (0,)), ((), ())), preferred_element_type=F32
            ))
        found = jnp.concatenate(found, axis=0)
        return found, (normalize(found) * gain[...]).astype(BF16)

    def columns(j, offset=0):
        return pl.ds(pl.multiple_of(j * wide_cols + offset, wide_cols), wide_cols)

    def project(rows_in, j, offset):
        return silu(jnp.dot(rows_in, win[:, columns(j, offset)], preferred_element_type=F32))

    def each_pair(step):
        def one(j, carry):
            step(j)
            return carry

        lax.fori_loop(0, HEADS // 2, one, 0)

    def attend(pieces, query_ref, event_user, emit):
        rows = sum(count for _, count in pieces) * pair_rows
        hidden = jnp.concatenate([
            recvb[pl.ds(first, count)].astype(F32).reshape(count * pair_rows, width)
            for first, count in pieces
        ], axis=0)
        normed[pl.ds(0, rows)] = (normalize(hidden) * gain[...]).astype(BF16)
        mask = row((cands, rows)) // per_user == event_user

        def pair(j):
            here = normed[pl.ds(0, rows)]
            keys = project(here, j, 2 * width).astype(BF16)
            vals = project(here, j, 3 * width).astype(BF16)
            query = query_ref[:, columns(j)]
            parts = []
            for h in range(2):
                part = slice(h * head, (h + 1) * head)
                scores = lax.dot_general(
                    query[:, part], keys[:, part], (((1,), (1,)), ((), ())),
                    preferred_element_type=F32,
                )
                weights = jnp.where(mask, silu(scores * head ** (-0.5)), 0.0).astype(BF16)
                parts.append(jnp.dot(weights, vals[:, part], preferred_element_type=F32))
            emit(j, jnp.concatenate(parts, axis=1))

        each_pair(pair)

    def arrive(first, last):
        def one(slot, carry):
            block_copy(slot, slot, slot).wait_recv()
            return carry

        lax.fori_loop(first, last, one, 0)

    def add(j, value):
        acc[:, columns(j)] += value

    ids_copy.wait_recv()
    found, normed_items = pool_items(0)
    items[...] = found.astype(BF16)

    def front(j):
        gate[:, columns(j)] = project(normed_items, j, 0)
        queries[:, columns(j)] = project(normed_items, j, width).astype(BF16)

    each_pair(front)
    acc[...] = jnp.zeros_like(acc)

    def attend_plane():
        arrive(1, quarter)
        attend([(0, quarter)], queries, by_event(own_table, quarter, lambda b: b), add)

    @pl.when(is_middle)
    def _():
        _, mate_items = pool_items(1)

        def ask(j):
            mate_queries[:, columns(j)] = project(mate_items, j, width).astype(BF16)

        each_pair(ask)
        far_users = by_event(by_slot(mate), half, lambda b: b)
        for i in range(1, STEPS - 1):
            turn(middle_step, i)
        arrive(half + 1, n)

        def emit(j, value):
            part_out[j] = value.astype(BF16)
            part_copy(j).start()

        attend([(half, half)], mate_queries, far_users, emit)
        turn(middle_step, STEPS - 1)
        attend_plane()
        arrive(quarter, half)
        attend(
            [(quarter, quarter)], queries,
            by_event(own_table, quarter, lambda b: b + quarter), add,
        )

        def join(j):
            part_copy(j).wait_recv()
            add(j, part_in[j].astype(F32))

        each_pair(join)

    @pl.when(jnp.logical_not(is_middle))
    def _():
        for i in range(STEPS):
            if i + 1 < STEPS:
                turn(end_step, i + 1)
            if i == 0:
                attend_plane()
            pieces = [(part * quarter + i * unit, unit) for part in range(1, 4)]
            for first, count in pieces:
                arrive(first, first + count)
            event_user = by_event(
                own_table, 3 * unit,
                lambda b: quarter * (1 + b // unit) + i * unit + b % unit,
            )
            attend(pieces, queries, event_user, add)

    gated = (normalize(acc[...]) * again[...] * gate[...]).astype(BF16)

    def last(j):
        total = jnp.dot(gated, wout[:, columns(j)], preferred_element_type=F32)
        out_ref[:, columns(j)] = (total + items[:, columns(j)].astype(F32)).astype(BF16)

    each_pair(last)

    ids_copy.wait_send()
    for stage in range(bits):
        pool_copy(stage).wait_send()

    run(False, 1, quarter - 1)

    @pl.when(is_middle)
    def _():
        run(False, half + quarter + 1, quarter - 1)
        middle_step(STEPS - 1, False)
        each_pair(lambda j: part_copy(j).wait_send())

    @pl.when(jnp.logical_not(is_middle))
    def _():
        end_step(STEPS - 1, False)


def body(n, history, pool, cand_ids, block_user, norm_gain, w_in, attn_gain, w_out):
    owned, block_rows, width = history.shape
    users_here, per_user = cand_ids.shape
    slot_count = max(1, 2 * owned // n)
    pair_rows = slot_count * block_rows
    shard_rows = pool.shape[0]
    bits = (n - 1).bit_length()
    cands = users_here * per_user
    pairs = (HEADS // 2, cands, 2 * width // HEADS)
    hbm = pl.BlockSpec(memory_space=pl.ANY)
    dma = pltpu.SemaphoreType.DMA
    out = pl.pallas_call(
        functools.partial(kernel, n, users_here, per_user, block_rows),
        out_shape=jax.ShapeDtypeStruct((cands, width), BF16),
        in_specs=[hbm] * 8,
        out_specs=pl.BlockSpec(memory_space=pltpu.VMEM),
        scratch_shapes=[
            pltpu.VMEM((owned * block_rows, width), BF16),
            pltpu.VMEM(w_in.shape, BF16),
            pltpu.VMEM(w_out.shape, BF16),
            pltpu.VMEM((1, width), F32),
            pltpu.VMEM((1, width), F32),
            pltpu.VMEM((2,) + cand_ids.shape, jnp.int32),
            pltpu.VMEM(block_user.shape, jnp.int32),
            pltpu.VMEM((n, pair_rows, width), BF16),
            pltpu.VMEM((n, pair_rows, width), BF16),
            pltpu.VMEM((n, shard_rows, width), BF16),
            pltpu.VMEM((cands, width), BF16),
            pltpu.VMEM((cands, width), BF16),
            pltpu.VMEM((cands, width), F32),
            pltpu.VMEM((cands, width), BF16),
            pltpu.VMEM((n // 2 * pair_rows, width), BF16),
            pltpu.VMEM((cands, width), F32),
            pltpu.VMEM(pairs, BF16),
            pltpu.VMEM(pairs, BF16),
            dma((8,)),
            dma((n,)),
            dma((n,)),
            dma((bits,)),
            dma((bits,)),
            dma((HEADS // 2,)),
            dma((HEADS // 2,)),
            dma((2,)),
        ],
        compiler_params=pltpu.CompilerParams(
            collective_id=0, has_side_effects=True, vmem_limit_bytes=56 * 1024 * 1024
        ),
    )(
        history.reshape(-1, width), pool, cand_ids, block_user, norm_gain.reshape(1, -1),
        attn_gain.reshape(1, -1), w_in, w_out,
    )
    return out.reshape(users_here, per_user, width)


def solution(mesh):
    in_specs = (
        P(("parts", "wide"), None, None),
        P(("parts", "wide"), None),
        P(("parts", "wide"), None),
        P("parts", None),
        P(),
        P(),
        P(),
        P(),
    )
    out_specs = P(("parts", "wide"), None, None)
    return jax.shard_map(
        functools.partial(body, mesh.shape["wide"]), mesh=mesh, in_specs=in_specs,
        out_specs=out_specs, check_vma=False,
    )
```

```python
import functools

import jax
import jax.numpy as jnp
from jax import lax
from jax.experimental import pallas as pl
from jax.experimental.pallas import tpu as pltpu
from jax.sharding import PartitionSpec as P

HEADS = 8
STEPS = 2
F32 = jnp.float32
BF16 = jnp.bfloat16


def silu(x, scale=1.0):
    half = (0.5 * scale) * x
    return half + half * jnp.tanh(half)


def normalize(values):
    average = jnp.mean(values, axis=-1, keepdims=True)
    centered = values - average
    spread = jnp.mean(centered * centered, axis=-1, keepdims=True)
    return centered * lax.rsqrt(spread + 1e-05)


def flip(me, step, bits):
    total = 0
    for k in range(bits):
        total = total + (1 << k) * ((me // (1 << k) + step // (1 << k)) % 2)
    return total


def lane(shape):
    return lax.broadcasted_iota(jnp.int32, shape, len(shape) - 1)


def row(shape):
    return lax.broadcasted_iota(jnp.int32, shape, 0)


def exact_dot(a, b):
    return jnp.dot(a, b, preferred_element_type=F32, precision=lax.Precision.HIGHEST)


def kernel(
    n, users_here, per_user, block_rows,
    hist_hbm, pool_hbm, ids_hbm, user_hbm, gain_hbm, again_hbm, win_hbm, wout_hbm,
    out_ref,
    hist, win, wout, gain, again, ids, block_user, sendb, recvb, poolb,
    queries, mate_queries, gate, items, normed, acc, part_out, part_in,
    local_sem, send_sem, recv_sem, pool_send, pool_recv, part_send, part_recv, ids_sem,
):
    bits = (n - 1).bit_length()
    half, quarter = n // 2, n // 4
    unit = quarter // STEPS
    me = lax.axis_index("wide")
    middle = (me // half + me // quarter) % 2
    is_middle = middle == 1
    mate = flip(me, half + quarter, bits)
    owned_rows, width = hist.shape
    owned = owned_rows // block_rows
    head = width // HEADS
    wide_cols = 2 * head
    pair_rows = sendb.shape[1]
    slots = pair_rows // block_rows
    cands = acc.shape[0]
    mesh_id = pl.DeviceIdType.MESH

    sources = (user_hbm, hist_hbm, pool_hbm, ids_hbm, gain_hbm, again_hbm, win_hbm, wout_hbm)
    places = (block_user, hist, poolb.at[0], ids.at[0], gain, again, win, wout)
    local = [
        pltpu.make_async_copy(source, place, local_sem.at[i])
        for i, (source, place) in enumerate(zip(sources, places))
    ]
    for copy in local:
        copy.start()

    barrier = pltpu.get_barrier_semaphore()

    def greet(step, carry):
        pl.semaphore_signal(
            barrier, inc=1, device_id={"wide": flip(me, step, bits)}, device_id_type=mesh_id
        )
        return carry

    lax.fori_loop(1, n, greet, 0)

    def block_copy(step, peer, slot):
        return pltpu.make_async_remote_copy(
            src_ref=sendb.at[step], dst_ref=recvb.at[slot],
            send_sem=send_sem.at[step], recv_sem=recv_sem.at[slot],
            device_id={"wide": flip(me, peer, bits)}, device_id_type=mesh_id,
        )

    def pool_copy(stage):
        count = 1 << stage
        return pltpu.make_async_remote_copy(
            src_ref=poolb.at[pl.ds(0, count)], dst_ref=poolb.at[pl.ds(count, count)],
            send_sem=pool_send.at[stage], recv_sem=pool_recv.at[stage],
            device_id={"wide": flip(me, 1 << (bits - 1 - stage), bits)}, device_id_type=mesh_id,
        )

    ids_copy = pltpu.make_async_remote_copy(
        src_ref=ids.at[0], dst_ref=ids.at[1], send_sem=ids_sem.at[0], recv_sem=ids_sem.at[1],
        device_id={"wide": mate}, device_id_type=mesh_id,
    )

    def part_copy(j):
        return pltpu.make_async_remote_copy(
            src_ref=part_out.at[j], dst_ref=part_in.at[j],
            send_sem=part_send.at[j], recv_sem=part_recv.at[j],
            device_id={"wide": mate}, device_id_type=mesh_id,
        )

    local[0].wait()
    users = block_user[...]
    targets = users // users_here
    mine = jnp.sum(jnp.where(row((n, owned)) == me, targets, 0), axis=0, keepdims=True)
    square = (owned, owned)
    mine_down = jnp.sum(jnp.where(row(square) == lane(square), mine, 0), axis=1, keepdims=True)
    earlier = row(square) < lane(square)
    within = jnp.sum(
        jnp.where((mine_down == mine) & earlier, 1, 0), axis=0, keepdims=True
    )
    position = flip(me, mine, bits) * slots + within
    spread_shape = (owned, owned_rows)
    spread = jnp.where(lane(spread_shape) // block_rows == row(spread_shape), 1.0, 0.0)
    position = exact_dot(jnp.broadcast_to(position.astype(F32), (8, owned)), spread)[:1]
    position = position.astype(jnp.int32) * block_rows + lane((1, owned_rows)) % block_rows
    for copy in local[1:4]:
        copy.wait()

    def pick(first, count):
        wanted = row((count * pair_rows, owned_rows)) + first * pair_rows
        chosen = jnp.where(wanted == position, 1.0, 0.0).astype(BF16)
        found = jnp.dot(chosen, hist[...], preferred_element_type=F32)
        sendb[pl.ds(first, count)] = found.reshape(count, pair_rows, width).astype(BF16)

    def run(act, first, count, peer_shift=0, slot_shift=0):
        def one(i, carry):
            copy = block_copy(first + i, first + i - peer_shift, first + i + slot_shift)
            copy.start() if act else copy.wait_send()
            return carry

        lax.fori_loop(0, count, one, 0)

    def end_step(i, act):
        if i < STEPS // 2:
            run(act, half + 2 * i * unit, 2 * unit, quarter, quarter)
        run(act, half + quarter + i * unit, unit)
        if i >= STEPS // 2:
            run(act, quarter + (2 * i - STEPS) * unit, 2 * unit)

    def middle_step(i, act):
        if i == 0:
            run(act, quarter, quarter)
        run(act, half + i * unit, unit)

    def turn(step, i):
        step(i - 1, False)
        step(i, True)

    pick(half, quarter)
    pick(half + quarter, quarter)
    pl.semaphore_wait(barrier, n - 1)
    pool_copy(0).start()
    ids_copy.start()
    pick(quarter, quarter)
    pool_copy(0).wait_recv()
    pool_copy(1).start()

    @pl.when(is_middle)
    def _():
        recvb[pl.ds(half, 1)] = sendb[pl.ds(half + quarter, 1)]

        run(True, half + quarter + 1, quarter - 1, half + quarter, -quarter)
        middle_step(0, True)

    @pl.when(jnp.logical_not(is_middle))
    def _():
        end_step(0, True)

    pick(0, quarter)
    recvb[pl.ds(0, 1)] = sendb[pl.ds(0, 1)]
    for stage in range(2, bits):
        pool_copy(stage - 1).wait_recv()
        pool_copy(stage).start()

    run(True, 1, quarter - 1)
    pool_copy(bits - 1).wait_recv()

    def by_slot(ranker):
        arrived = targets == ranker
        count = exact_dot(jnp.where(arrived, 1.0, 0.0), jnp.where(earlier, 1.0, 0.0))
        count = count.astype(jnp.int32)
        label = users - ranker * users_here + 1
        return [
            jnp.sum(jnp.where(arrived & (count == slot), label, 0), axis=1, keepdims=True)
            for slot in range(slots)
        ]

    def by_event(table, blocks, step_of):
        shape = (n, blocks * pair_rows)
        slot_here = (lane(shape) % pair_rows) // block_rows
        owner = flip(me, step_of(lane((1, shape[1])) // pair_rows), bits)
        total = jnp.zeros(shape, jnp.int32)
        for slot in range(slots):
            total = total + jnp.where(slot_here == slot, table[slot], 0)
        return jnp.sum(jnp.where(row(shape) == owner, total, 0), axis=0, keepdims=True) - 1

    own_table = by_slot(me)

    shards, shard_rows, _ = poolb.shape
    pool_rows = shards * shard_rows
    for copy in local[4:]:
        copy.wait()

    def pool_items(which):
        wanted = ids[which]
        relative = flip(me, wanted // shard_rows, bits)
        place = jnp.zeros_like(relative)
        for k in range(bits):
            place = place + ((relative // (1 << k)) % 2) * (1 << (bits - 1 - k))
        place = place * shard_rows + wanted % shard_rows
        table = poolb[...].astype(F32).reshape(pool_rows, width).astype(BF16)
        found = []
        for u in range(users_here):
            chosen = jnp.where(row((pool_rows, per_user)) == place[u:u + 1], 1.0, 0.0).astype(BF16)
            found.append(lax.dot_general(
                chosen, table, (((0,), (0,)), ((), ())), preferred_element_type=F32
            ))
        found = jnp.concatenate(found, axis=0)
        return found, (normalize(found) * gain[...]).astype(BF16)

    def columns(j, offset=0):
        return pl.ds(pl.multiple_of(j * wide_cols + offset, wide_cols), wide_cols)

    def project(rows_in, j, offset):
        return silu(jnp.dot(rows_in, win[:, columns(j, offset)], preferred_element_type=F32))

    def each_pair(step, unroll=1):
        def one(j, carry):
            step(j)
            return carry

        lax.fori_loop(0, HEADS // 2, one, 0, unroll=unroll)

    def attend(pieces, query_ref, event_user, emit):
        rows = sum(count for _, count in pieces) * pair_rows
        hidden = jnp.concatenate([
            recvb[pl.ds(first, count)].astype(F32).reshape(count * pair_rows, width)
            for first, count in pieces
        ], axis=0)
        normed[pl.ds(0, rows)] = (normalize(hidden) * gain[...]).astype(BF16)
        mask = row((cands, rows)) // per_user == event_user

        def pair(j):
            here = normed[pl.ds(0, rows)]
            keys = project(here, j, 2 * width).astype(BF16)
            vals = project(here, j, 3 * width).astype(BF16)
            query = query_ref[:, columns(j)]
            parts = []
            for h in range(2):
                part = slice(h * head, (h + 1) * head)
                scores = lax.dot_general(
                    query[:, part], keys[:, part], (((1,), (1,)), ((), ())),
                    preferred_element_type=F32,
                )
                weights = jnp.where(mask, silu(scores, head ** (-0.5)), 0.0).astype(BF16)
                parts.append(jnp.dot(weights, vals[:, part], preferred_element_type=F32))
            emit(j, jnp.concatenate(parts, axis=1))

        each_pair(pair, unroll=2)

    def arrive(first, last):
        def one(slot, carry):
            block_copy(slot, slot, slot).wait_recv()
            return carry

        lax.fori_loop(first, last, one, 0)

    def add(j, value):
        acc[:, columns(j)] += value

    ids_copy.wait_recv()
    found, normed_items = pool_items(0)
    items[...] = found.astype(BF16)

    def front(j):
        gate[:, columns(j)] = project(normed_items, j, 0)
        queries[:, columns(j)] = project(normed_items, j, width).astype(BF16)

    each_pair(front)
    acc[...] = jnp.zeros_like(acc)

    def attend_plane():
        arrive(1, quarter)
        attend([(0, quarter)], queries, by_event(own_table, quarter, lambda b: b), add)

    def attend_near():
        arrive(quarter, half)
        event_user = by_event(own_table, quarter, lambda b: b + quarter)
        attend([(quarter, quarter)], queries, event_user, add)

    @pl.when(is_middle)
    def _():
        _, mate_items = pool_items(1)

        def ask(j):
            mate_queries[:, columns(j)] = project(mate_items, j, width).astype(BF16)

        each_pair(ask)
        far_users = by_event(by_slot(mate), half, lambda b: b)
        for i in range(1, STEPS):
            turn(middle_step, i)
        arrive(half + 1, n)

        def emit(j, value):
            part_out[j] = value.astype(BF16)
            part_copy(j).start()

        attend([(half, half)], mate_queries, far_users, emit)
        attend_plane()
        attend_near()

        def join(j):
            part_copy(j).wait_recv()
            add(j, part_in[j].astype(F32))

        each_pair(join)

    @pl.when(jnp.logical_not(is_middle))
    def _():
        for i in range(STEPS):
            if i + 1 < STEPS:
                turn(end_step, i + 1)
            if i == 0:
                attend_plane()
                attend_near()
            pieces = [(part * quarter + i * unit, unit) for part in range(2, 4)]
            for first, count in pieces:
                arrive(first, first + count)
            event_user = by_event(
                own_table, 2 * unit,
                lambda b: quarter * (2 + b // unit) + i * unit + b % unit,
            )
            attend(pieces, queries, event_user, add)

    gated = (normalize(acc[...]) * again[...] * gate[...]).astype(BF16)

    def last(j):
        total = jnp.dot(gated, wout[:, columns(j)], preferred_element_type=F32)
        out_ref[:, columns(j)] = (total + items[:, columns(j)].astype(F32)).astype(BF16)

    each_pair(last)

    ids_copy.wait_send()
    for stage in range(bits):
        pool_copy(stage).wait_send()

    run(False, 1, quarter - 1)

    @pl.when(is_middle)
    def _():
        run(False, half + quarter + 1, quarter - 1)
        middle_step(STEPS - 1, False)
        each_pair(lambda j: part_copy(j).wait_send())

    @pl.when(jnp.logical_not(is_middle))
    def _():
        end_step(STEPS - 1, False)


def body(n, history, pool, cand_ids, block_user, norm_gain, w_in, attn_gain, w_out):
    owned, block_rows, width = history.shape
    users_here, per_user = cand_ids.shape
    slot_count = max(1, 2 * owned // n)
    pair_rows = slot_count * block_rows
    shard_rows = pool.shape[0]
    bits = (n - 1).bit_length()
    cands = users_here * per_user
    pairs = (HEADS // 2, cands, 2 * width // HEADS)
    hbm = pl.BlockSpec(memory_space=pl.ANY)
    dma = pltpu.SemaphoreType.DMA
    out = pl.pallas_call(
        functools.partial(kernel, n, users_here, per_user, block_rows),
        out_shape=jax.ShapeDtypeStruct((cands, width), BF16),
        in_specs=[hbm] * 8,
        out_specs=pl.BlockSpec(memory_space=pltpu.VMEM),
        scratch_shapes=[
            pltpu.VMEM((owned * block_rows, width), BF16),
            pltpu.VMEM(w_in.shape, BF16),
            pltpu.VMEM(w_out.shape, BF16),
            pltpu.VMEM((1, width), F32),
            pltpu.VMEM((1, width), F32),
            pltpu.VMEM((2,) + cand_ids.shape, jnp.int32),
            pltpu.VMEM(block_user.shape, jnp.int32),
            pltpu.VMEM((n, pair_rows, width), BF16),
            pltpu.VMEM((n, pair_rows, width), BF16),
            pltpu.VMEM((n, shard_rows, width), BF16),
            pltpu.VMEM((cands, width), BF16),
            pltpu.VMEM((cands, width), BF16),
            pltpu.VMEM((cands, width), F32),
            pltpu.VMEM((cands, width), BF16),
            pltpu.VMEM((n // 2 * pair_rows, width), BF16),
            pltpu.VMEM((cands, width), F32),
            pltpu.VMEM(pairs, BF16),
            pltpu.VMEM(pairs, BF16),
            dma((8,)),
            dma((n,)),
            dma((n,)),
            dma((bits,)),
            dma((bits,)),
            dma((HEADS // 2,)),
            dma((HEADS // 2,)),
            dma((2,)),
        ],
        compiler_params=pltpu.CompilerParams(
            collective_id=0, has_side_effects=True, vmem_limit_bytes=56 * 1024 * 1024
        ),
    )(
        history.reshape(-1, width), pool, cand_ids, block_user, norm_gain.reshape(1, -1),
        attn_gain.reshape(1, -1), w_in, w_out,
    )
    return out.reshape(users_here, per_user, width)


def solution(mesh):
    in_specs = (
        P(("parts", "wide"), None, None),
        P(("parts", "wide"), None),
        P(("parts", "wide"), None),
        P("parts", None),
        P(),
        P(),
        P(),
        P(),
    )
    out_specs = P(("parts", "wide"), None, None)
    return jax.shard_map(
        functools.partial(body, mesh.shape["wide"]), mesh=mesh, in_specs=in_specs,
        out_specs=out_specs, check_vma=False,
    )
```

```python
import functools

import jax
import jax.numpy as jnp
from jax import lax
from jax.experimental import pallas as pl
from jax.experimental.pallas import tpu as pltpu
from jax.sharding import PartitionSpec as P

HEADS = 8
STEPS = 2
F32 = jnp.float32
BF16 = jnp.bfloat16


def silu(x, scale=1.0):
    half = (0.5 * scale) * x
    return half + half * jnp.tanh(half)


def normalize(values):
    average = jnp.mean(values, axis=-1, keepdims=True)
    centered = values - average
    spread = jnp.mean(centered * centered, axis=-1, keepdims=True)
    return centered * lax.rsqrt(spread + 1e-05)


def flip(me, step, bits):
    total = 0
    for k in range(bits):
        total = total + (1 << k) * ((me // (1 << k) + step // (1 << k)) % 2)
    return total


def lane(shape):
    return lax.broadcasted_iota(jnp.int32, shape, len(shape) - 1)


def row(shape):
    return lax.broadcasted_iota(jnp.int32, shape, 0)


def exact_dot(a, b):
    return jnp.dot(a, b, preferred_element_type=F32, precision=lax.Precision.HIGHEST)


def kernel(
    n, users_here, per_user, block_rows,
    hist_hbm, pool_hbm, ids_hbm, user_hbm, gain_hbm, again_hbm, win_hbm, wout_hbm,
    out_ref,
    hist, win, wout, gain, again, ids, block_user, sendb, recvb, poolb,
    queries, mate_queries, gate, items, normed, acc, part_out, part_in,
    local_sem, send_sem, recv_sem, pool_send, pool_recv, part_send, part_recv, ids_sem,
):
    bits = (n - 1).bit_length()
    half, quarter = n // 2, n // 4
    unit = quarter // STEPS
    me = lax.axis_index("wide")
    middle = (me // half + me // quarter) % 2
    is_middle = middle == 1
    mate = flip(me, half + quarter, bits)
    owned_rows, width = hist.shape
    owned = owned_rows // block_rows
    head = width // HEADS
    wide_cols = 2 * head
    pair_rows = sendb.shape[1]
    slots = pair_rows // block_rows
    cands = acc.shape[0]
    mesh_id = pl.DeviceIdType.MESH

    sources = (user_hbm, hist_hbm, pool_hbm, ids_hbm, gain_hbm, again_hbm, win_hbm, wout_hbm)
    places = (block_user, hist, poolb.at[0], ids.at[0], gain, again, win, wout)
    local = [
        pltpu.make_async_copy(source, place, local_sem.at[i])
        for i, (source, place) in enumerate(zip(sources, places))
    ]
    for copy in local:
        copy.start()

    barrier = pltpu.get_barrier_semaphore()

    def greet(step, carry):
        pl.semaphore_signal(
            barrier, inc=1, device_id={"wide": flip(me, step, bits)}, device_id_type=mesh_id
        )
        return carry

    lax.fori_loop(1, n, greet, 0)

    def block_copy(step, peer, slot):
        return pltpu.make_async_remote_copy(
            src_ref=sendb.at[step], dst_ref=recvb.at[slot],
            send_sem=send_sem.at[step], recv_sem=recv_sem.at[slot],
            device_id={"wide": flip(me, peer, bits)}, device_id_type=mesh_id,
        )

    def pool_copy(stage):
        count = 1 << stage
        return pltpu.make_async_remote_copy(
            src_ref=poolb.at[pl.ds(0, count)], dst_ref=poolb.at[pl.ds(count, count)],
            send_sem=pool_send.at[stage], recv_sem=pool_recv.at[stage],
            device_id={"wide": flip(me, 1 << (bits - 1 - stage), bits)}, device_id_type=mesh_id,
        )

    ids_copy = pltpu.make_async_remote_copy(
        src_ref=ids.at[0], dst_ref=ids.at[1], send_sem=ids_sem.at[0], recv_sem=ids_sem.at[1],
        device_id={"wide": mate}, device_id_type=mesh_id,
    )

    def part_copy(j):
        return pltpu.make_async_remote_copy(
            src_ref=part_out.at[j], dst_ref=part_in.at[j],
            send_sem=part_send.at[j], recv_sem=part_recv.at[j],
            device_id={"wide": mate}, device_id_type=mesh_id,
        )

    local[0].wait()
    users = block_user[...]
    targets = users // users_here
    mine = jnp.sum(jnp.where(row((n, owned)) == me, targets, 0), axis=0, keepdims=True)
    square = (owned, owned)
    mine_down = jnp.sum(jnp.where(row(square) == lane(square), mine, 0), axis=1, keepdims=True)
    earlier = row(square) < lane(square)
    within = jnp.sum(
        jnp.where((mine_down == mine) & earlier, 1, 0), axis=0, keepdims=True
    )
    position = flip(me, mine, bits) * slots + within
    spread_shape = (owned, owned_rows)
    spread = jnp.where(lane(spread_shape) // block_rows == row(spread_shape), 1.0, 0.0)
    position = exact_dot(jnp.broadcast_to(position.astype(F32), (8, owned)), spread)[:1]
    position = position.astype(jnp.int32) * block_rows + lane((1, owned_rows)) % block_rows
    for copy in local[1:4]:
        copy.wait()

    def pick(first, count):
        wanted = row((count * pair_rows, owned_rows)) + first * pair_rows
        chosen = jnp.where(wanted == position, 1.0, 0.0).astype(BF16)
        found = jnp.dot(chosen, hist[...], preferred_element_type=F32)
        sendb[pl.ds(first, count)] = found.reshape(count, pair_rows, width).astype(BF16)

    def run(act, first, count, peer_shift=0, slot_shift=0):
        def one(i, carry):
            copy = block_copy(first + i, first + i - peer_shift, first + i + slot_shift)
            copy.start() if act else copy.wait_send()
            return carry

        lax.fori_loop(0, count, one, 0)

    def end_step(i, act):
        if i < STEPS // 2:
            run(act, half + 2 * i * unit, 2 * unit, quarter, quarter)
        run(act, half + quarter + i * unit, unit)
        if i >= STEPS // 2:
            run(act, quarter + (2 * i - STEPS) * unit, 2 * unit)

    def middle_sends(act):
        run(act, quarter, 2 * quarter)

    def turn(step, i):
        step(i - 1, False)
        step(i, True)

    pick(half, quarter)
    pick(half + quarter, quarter)
    pl.semaphore_wait(barrier, n - 1)
    pool_copy(0).start()
    ids_copy.start()
    pick(quarter, quarter)
    pool_copy(0).wait_recv()
    pool_copy(1).start()

    @pl.when(is_middle)
    def _():
        recvb[pl.ds(half, 1)] = sendb[pl.ds(half + quarter, 1)]

        run(True, half + quarter + 1, quarter - 1, half + quarter, -quarter)
        middle_sends(True)

    @pl.when(jnp.logical_not(is_middle))
    def _():
        end_step(0, True)

    pick(0, quarter)
    recvb[pl.ds(0, 1)] = sendb[pl.ds(0, 1)]
    for stage in range(2, bits):
        pool_copy(stage - 1).wait_recv()
        pool_copy(stage).start()

    run(True, 1, quarter - 1)
    pool_copy(bits - 1).wait_recv()

    def by_slot(ranker):
        arrived = targets == ranker
        count = exact_dot(jnp.where(arrived, 1.0, 0.0), jnp.where(earlier, 1.0, 0.0))
        count = count.astype(jnp.int32)
        label = users - ranker * users_here + 1
        return [
            jnp.sum(jnp.where(arrived & (count == slot), label, 0), axis=1, keepdims=True)
            for slot in range(slots)
        ]

    def by_event(table, blocks, step_of):
        shape = (n, blocks * pair_rows)
        slot_here = (lane(shape) % pair_rows) // block_rows
        owner = flip(me, step_of(lane((1, shape[1])) // pair_rows), bits)
        total = jnp.zeros(shape, jnp.int32)
        for slot in range(slots):
            total = total + jnp.where(slot_here == slot, table[slot], 0)
        return jnp.sum(jnp.where(row(shape) == owner, total, 0), axis=0, keepdims=True) - 1

    own_table = by_slot(me)

    shards, shard_rows, _ = poolb.shape
    pool_rows = shards * shard_rows
    for copy in local[4:]:
        copy.wait()

    def pool_items(which):
        wanted = ids[which]
        relative = flip(me, wanted // shard_rows, bits)
        place = jnp.zeros_like(relative)
        for k in range(bits):
            place = place + ((relative // (1 << k)) % 2) * (1 << (bits - 1 - k))
        place = place * shard_rows + wanted % shard_rows
        table = poolb[...].astype(F32).reshape(pool_rows, width).astype(BF16)
        found = []
        for u in range(users_here):
            chosen = jnp.where(row((pool_rows, per_user)) == place[u:u + 1], 1.0, 0.0).astype(BF16)
            found.append(lax.dot_general(
                chosen, table, (((0,), (0,)), ((), ())), preferred_element_type=F32
            ))
        found = jnp.concatenate(found, axis=0)
        return found, (normalize(found) * gain[...]).astype(BF16)

    def columns(j, offset=0):
        return pl.ds(pl.multiple_of(j * wide_cols + offset, wide_cols), wide_cols)

    def project(rows_in, j, offset):
        return silu(jnp.dot(rows_in, win[:, columns(j, offset)], preferred_element_type=F32))

    def each_pair(step, unroll=1):
        def one(j, carry):
            step(j)
            return carry

        lax.fori_loop(0, HEADS // 2, one, 0, unroll=unroll)

    def attend(pieces, query_ref, event_user, emit):
        rows = sum(count for _, count in pieces) * pair_rows
        hidden = jnp.concatenate([
            recvb[pl.ds(first, count)].astype(F32).reshape(count * pair_rows, width)
            for first, count in pieces
        ], axis=0)
        normed[pl.ds(0, rows)] = (normalize(hidden) * gain[...]).astype(BF16)
        mask = row((cands, rows)) // per_user == event_user

        def pair(j):
            here = normed[pl.ds(0, rows)]
            keys = project(here, j, 2 * width).astype(BF16)
            vals = project(here, j, 3 * width).astype(BF16)
            query = query_ref[:, columns(j)]
            parts = []
            for h in range(2):
                part = slice(h * head, (h + 1) * head)
                scores = lax.dot_general(
                    query[:, part], keys[:, part], (((1,), (1,)), ((), ())),
                    preferred_element_type=F32,
                )
                weights = jnp.where(mask, silu(scores, head ** (-0.5)), 0.0).astype(BF16)
                parts.append(jnp.dot(weights, vals[:, part], preferred_element_type=F32))
            emit(j, jnp.concatenate(parts, axis=1))

        each_pair(pair, unroll=2)

    def arrive(first, last):
        def one(slot, carry):
            block_copy(slot, slot, slot).wait_recv()
            return carry

        lax.fori_loop(first, last, one, 0)

    def add(j, value):
        acc[:, columns(j)] += value

    ids_copy.wait_recv()
    found, normed_items = pool_items(0)
    items[...] = found.astype(BF16)

    def front(j):
        gate[:, columns(j)] = project(normed_items, j, 0)
        queries[:, columns(j)] = project(normed_items, j, width).astype(BF16)

    each_pair(front)
    acc[...] = jnp.zeros_like(acc)

    def attend_plane():
        arrive(1, quarter)
        attend([(0, quarter)], queries, by_event(own_table, quarter, lambda b: b), add)

    def attend_near():
        arrive(quarter, half)
        event_user = by_event(own_table, quarter, lambda b: b + quarter)
        attend([(quarter, quarter)], queries, event_user, add)

    @pl.when(is_middle)
    def _():
        _, mate_items = pool_items(1)

        def ask(j):
            mate_queries[:, columns(j)] = project(mate_items, j, width).astype(BF16)

        each_pair(ask)
        far_users = by_event(by_slot(mate), half, lambda b: b)
        arrive(half + 1, n)

        def emit(j, value):
            part_out[j] = value.astype(BF16)
            part_copy(j).start()

        attend([(half, half)], mate_queries, far_users, emit)
        attend_plane()
        attend_near()

        def join(j):
            part_copy(j).wait_recv()
            add(j, part_in[j].astype(F32))

        each_pair(join)

    @pl.when(jnp.logical_not(is_middle))
    def _():
        for i in range(STEPS):
            if i + 1 < STEPS:
                turn(end_step, i + 1)
            if i == 0:
                attend_plane()
                attend_near()
            pieces = [(part * quarter + i * unit, unit) for part in range(2, 4)]
            for first, count in pieces:
                arrive(first, first + count)
            event_user = by_event(
                own_table, 2 * unit,
                lambda b: quarter * (2 + b // unit) + i * unit + b % unit,
            )
            attend(pieces, queries, event_user, add)

    gated = (normalize(acc[...]) * again[...] * gate[...]).astype(BF16)

    def last(j):
        total = jnp.dot(gated, wout[:, columns(j)], preferred_element_type=F32)
        out_ref[:, columns(j)] = (total + items[:, columns(j)].astype(F32)).astype(BF16)

    each_pair(last)

    ids_copy.wait_send()
    for stage in range(bits):
        pool_copy(stage).wait_send()

    run(False, 1, quarter - 1)

    @pl.when(is_middle)
    def _():
        run(False, half + quarter + 1, quarter - 1)
        middle_sends(False)
        each_pair(lambda j: part_copy(j).wait_send())

    @pl.when(jnp.logical_not(is_middle))
    def _():
        end_step(STEPS - 1, False)


def body(n, history, pool, cand_ids, block_user, norm_gain, w_in, attn_gain, w_out):
    owned, block_rows, width = history.shape
    users_here, per_user = cand_ids.shape
    slot_count = max(1, 2 * owned // n)
    pair_rows = slot_count * block_rows
    shard_rows = pool.shape[0]
    bits = (n - 1).bit_length()
    cands = users_here * per_user
    pairs = (HEADS // 2, cands, 2 * width // HEADS)
    hbm = pl.BlockSpec(memory_space=pl.ANY)
    dma = pltpu.SemaphoreType.DMA
    out = pl.pallas_call(
        functools.partial(kernel, n, users_here, per_user, block_rows),
        out_shape=jax.ShapeDtypeStruct((cands, width), BF16),
        in_specs=[hbm] * 8,
        out_specs=pl.BlockSpec(memory_space=pltpu.VMEM),
        scratch_shapes=[
            pltpu.VMEM((owned * block_rows, width), BF16),
            pltpu.VMEM(w_in.shape, BF16),
            pltpu.VMEM(w_out.shape, BF16),
            pltpu.VMEM((1, width), F32),
            pltpu.VMEM((1, width), F32),
            pltpu.VMEM((2,) + cand_ids.shape, jnp.int32),
            pltpu.VMEM(block_user.shape, jnp.int32),
            pltpu.VMEM((n, pair_rows, width), BF16),
            pltpu.VMEM((n, pair_rows, width), BF16),
            pltpu.VMEM((n, shard_rows, width), BF16),
            pltpu.VMEM((cands, width), BF16),
            pltpu.VMEM((cands, width), BF16),
            pltpu.VMEM((cands, width), F32),
            pltpu.VMEM((cands, width), BF16),
            pltpu.VMEM((n // 2 * pair_rows, width), BF16),
            pltpu.VMEM((cands, width), F32),
            pltpu.VMEM(pairs, BF16),
            pltpu.VMEM(pairs, BF16),
            dma((8,)),
            dma((n,)),
            dma((n,)),
            dma((bits,)),
            dma((bits,)),
            dma((HEADS // 2,)),
            dma((HEADS // 2,)),
            dma((2,)),
        ],
        compiler_params=pltpu.CompilerParams(
            collective_id=0, has_side_effects=True, vmem_limit_bytes=56 * 1024 * 1024
        ),
    )(
        history.reshape(-1, width), pool, cand_ids, block_user, norm_gain.reshape(1, -1),
        attn_gain.reshape(1, -1), w_in, w_out,
    )
    return out.reshape(users_here, per_user, width)


def solution(mesh):
    in_specs = (
        P(("parts", "wide"), None, None),
        P(("parts", "wide"), None),
        P(("parts", "wide"), None),
        P("parts", None),
        P(),
        P(),
        P(),
        P(),
    )
    out_specs = P(("parts", "wide"), None, None)
    return jax.shard_map(
        functools.partial(body, mesh.shape["wide"]), mesh=mesh, in_specs=in_specs,
        out_specs=out_specs, check_vma=False,
    )
```
